256 devices in a mesh: pipe: 8 (over y, x_lo), expert: 16 (over x_hi, z), dp: 2 (over core).
Axes of the slice: x: 4 (x_hi: 2, x_lo: 2; x = x_hi * 2 + x_lo), y: 4, z: 8, core: 2. Of those that a mesh axis runs over, the one named last changes fastest.
Arguments:
- inputs: bfloat16 [8, 2, 4096, 2048], P('pipe', None, ('expert', 'dp')), may hold values from -6 to 6
- upstream: bfloat16 [8, 2, 4096, 2048], P('pipe', None, ('expert', 'dp')), may hold values from -6 to 6
- routes: int32 [8, 2, 4096, 8], P('pipe', None, ('expert', 'dp')), may hold values from 0 to 127, all different within a row; in each aligned block of 128 rows (0 to 127, 128 to 255, ..., all dimensions but the last counted through in order) at most 24 rows name the same one
- gate_weights: bfloat16 [8, 2, 4096, 8], P('pipe', None, ('expert', 'dp')), may hold values from 0.5 to 2
- proj_in: bfloat16 [8, 16, 2048, 768], P('pipe', 'expert'), may hold values from -0.125 to 0.125
- proj_out: bfloat16 [8, 16, 768, 2048], P('pipe', 'expert'), may hold values from -0.21875 to 0.21875
Outputs:
- prev_grad: bfloat16 [8, 2, 4096, 2048], P('pipe', None, ('expert', 'dp'))
- proj_out_grad: bfloat16 [8, 16, 768, 2048], P('pipe', 'expert')
The draws below stay inside these ranges and needn't reach their ends.
Inputs may be any that keep to these rules, and one draw needn't show every extreme that they name: `routes`: in each aligned block of 128 rows (one device's tokens of one section and micro-batch) no expert is named by more than 24 rows; the experts of one row differ.
All inputs are finite; a program needn't handle non-finite values.
Results may differ from the reference program's by a relative error of at most 0.0062.
Values may be sent and summed in bfloat16 or wider, within the bound.
No kernel may reach another device: no remote copies, remote signals or barrier semaphores. Data moves between devices by JAX's collectives and lax.ppermute only.
A program may use at most 128 MiB of HBM per device.

```python
import math
import jax
import jax.numpy as jnp
import numpy as np
from jax import lax

D = 2048
HID = 768
EXPERTS = 128
TOP = 8
MICRO = 2
TOK_DEV = 128
CAP = 24
SECTIONS = 8
GROUPS = 16
EXP_LOCAL = 8
TOKENS = 4096
N_EXPERT = 16
N_DP = 2


def block_scale(stream_key, extent, cuts, least, top_value):
    loudness = 1.0
    for position, blocks in cuts:
        draws = jax.random.uniform(jax.random.fold_in(jax.random.fold_in(stream_key, 6), position), (blocks,), jnp.float32, least / len(cuts), top_value / len(cuts))
        loudness = loudness * jnp.repeat(jnp.exp(draws), extent[position] // blocks).reshape((-1,) + (1,) * (len(extent) - 1 - position))
    return loudness


def deal_out(key, own, number, rows, count, top, bound, skew):
    ranking = jax.random.permutation(key, count)
    heavy_load, common = load_shares(count, rows * top, bound, skew, True), load_shares(count, rows * top, bound, skew, False)
    places = jnp.arange(count)

    def named(sizes, rotation):
        used = int((sizes > 0).sum())
        fixed = max(1, used // 4)
        moved = fixed + (places - fixed + rotation * (used - fixed)) % max(1, count - fixed)
        return jnp.zeros((count,), jnp.int32).at[ranking[jnp.where(places < fixed, places, moved)]].set(jnp.asarray(sizes, jnp.int32))

    sizes = jnp.where(number % 4 == 0, named(heavy_load, number // 4), named(common, number - number // 4 - 1))
    mixed = jax.random.permutation(jax.random.fold_in(own, 3), count)
    giver, taker = mixed[0:count // 2 * 2:2], mixed[1:count // 2 * 2:2]
    slack = jnp.minimum(sizes[giver] - 1, bound - sizes[taker]) // 2
    slack = jnp.where((giver == ranking[0]) | (taker == ranking[0]) | (sizes[taker] == 0), 0, jnp.maximum(slack, 0))
    moved = jax.random.randint(jax.random.fold_in(own, 4), (count // 2,), 0, 1 << 20) % (slack + 1)
    sizes = sizes.at[giver].add(-moved).at[taker].add(moved)
    labels = jnp.searchsorted(jnp.cumsum(sizes), jnp.arange(rows * top), side="right").astype(jnp.int32)
    grid = labels.reshape(top, rows).T
    grid = grid[jax.random.permutation(jax.random.fold_in(own, 1), rows)]
    rotation = jax.random.randint(jax.random.fold_in(own, 2), (rows, 1), 0, top)
    return jnp.take_along_axis(grid, (jnp.arange(top)[None, :] + rotation) % top, axis=1)


def load_shares(count, total, reach, skew, full):
    loads = [(1 << 20) // math.isqrt(rank ** skew) + 1 for rank in range(1, count + 1)]
    largest = reach if full else min(reach, max(-(-total // count), total * loads[0] // sum(loads)))
    least = 1 if total - largest >= count - 1 else 0
    given, spare = [largest] + [least] * (count - 1), total - largest - least * (count - 1)
    while spare > 0:
        candidates = [i for i in range(1, count) if given[i] < largest] or [i for i in range(1, count) if given[i] < reach]
        whole, budget = sum([loads[i] for i in candidates]), spare
        for i in candidates:
            addition = min(reach - given[i], max(1, budget * loads[i] // whole), spare)
            given[i] = given[i] + addition
            spare = spare - addition
    return np.array(given)


def normal_values(rng, dims, spread, bound, shards=(), kind=jnp.bfloat16):
    drawn = spread * jax.random.normal(rng, dims, jnp.float32)
    if shards:
        drawn = drawn * block_scale(rng, dims, shards, -0.22, 0.18)
    return jnp.clip(drawn, -bound, bound).astype(kind)


def setup_inputs(seed: int = 0) -> dict:
    streams_of = jax.random.split(jax.random.key(seed), 7)
    inputs = normal_values(streams_of[0], (SECTIONS, MICRO, TOKENS, D), 1.0, 6.0, ((0, 8), (2, 32)))
    upstream = normal_values(streams_of[1], (SECTIONS, MICRO, TOKENS, D), 1.0, 6.0, ((0, 8), (2, 32)))
    routes_keys = jax.random.split(jax.random.fold_in(streams_of[2], 1), SECTIONS * MICRO * TOKENS // TOK_DEV)
    routes_turns = jax.random.permutation(jax.random.fold_in(streams_of[2], 3), SECTIONS * MICRO * TOKENS // TOK_DEV)
    routes = jax.vmap(lambda own, number: deal_out(jax.random.fold_in(streams_of[2], 2), own, number, TOK_DEV, EXPERTS, TOP, CAP, 2))(routes_keys, routes_turns).reshape((SECTIONS, MICRO, TOKENS, TOP))
    gate_weights = jnp.clip(0.5 + 1.5 * jax.random.uniform(streams_of[3], (SECTIONS, MICRO, TOKENS, TOP), jnp.float32) ** block_scale(streams_of[3], (SECTIONS, MICRO, TOKENS, TOP), ((0, 8), (2, 32)), -0.2, 0.2), 0.5, 2.0).astype(jnp.bfloat16)
    proj_in = normal_values(streams_of[4], (SECTIONS, GROUPS, D, HID), D ** -0.5, 0.125, ((0, 8), (1, 16)))
    proj_out = normal_values(streams_of[5], (SECTIONS, GROUPS, HID, D), HID ** -0.5, 0.21875, ((0, 8), (1, 16)))
    return {"inputs": inputs, "upstream": upstream, "routes": routes, "gate_weights": gate_weights, "proj_in": proj_in, "proj_out": proj_out}


def expert_rows(rows_in, rows_grad, rows_gate, weight_in, weight_out):
    scaled = (rows_gate.astype(jnp.float32)[:, None] * rows_grad.astype(jnp.float32)).astype(jnp.bfloat16)
    pre_act = jnp.dot(rows_in, weight_in, preferred_element_type=jnp.float32)
    sigmoid = jax.nn.sigmoid(pre_act)
    hidden = (pre_act * sigmoid).astype(jnp.bfloat16)
    hidden_grad = jnp.dot(scaled, weight_out.T, preferred_element_type=jnp.float32)
    pre_grad = (hidden_grad * sigmoid * (1.0 + pre_act * (1.0 - sigmoid))).astype(jnp.bfloat16)
    returned = jnp.dot(pre_grad, weight_in.T, preferred_element_type=jnp.float32).astype(jnp.bfloat16)
    partial_value = jnp.dot(hidden.T, scaled, preferred_element_type=jnp.float32)
    return returned, partial_value


def reference(inputs, upstream, routes, gate_weights, proj_in, proj_out):
    blocks = N_EXPERT * N_DP
    targets = jnp.arange(GROUPS, dtype=jnp.int32) * EXP_LOCAL
    slot_ids = jnp.arange(CAP, dtype=jnp.int32)
    section_grads = []
    weight_grads = []
    for section_idx in range(SECTIONS):
        section_sum = jnp.zeros((GROUPS, HID, D), jnp.float32)
        micro_list = []
        for micro_idx in range(MICRO):
            rows_in = inputs[section_idx, micro_idx].reshape(blocks, TOK_DEV, D)
            rows_grad = upstream[section_idx, micro_idx].reshape(blocks, TOK_DEV, D)
            route_ids = routes[section_idx, micro_idx].reshape(blocks, TOK_DEV, TOP)
            gate_rows = gate_weights[section_idx, micro_idx].reshape(blocks, TOK_DEV, TOP).astype(jnp.float32)
            matches = route_ids[:, :, :, None] == targets
            routed = jnp.any(matches, axis=2)
            weight = jnp.sum(jnp.where(matches, gate_rows[:, :, :, None], 0.0), axis=2)
            slot_rank = jnp.cumsum(routed.astype(jnp.int32), axis=1) - 1
            placing = (routed[..., None] & (slot_rank[..., None] == slot_ids)).astype(jnp.float32)
            send_in = jnp.einsum("btnc,btd->nbcd", placing, rows_in.astype(jnp.float32)).astype(jnp.bfloat16)
            send_grad = jnp.einsum("btnc,btd->nbcd", placing, rows_grad.astype(jnp.float32)).astype(jnp.bfloat16)
            send_gate = jnp.einsum("btnc,btn->nbc", placing, weight).astype(jnp.bfloat16)

            def one_group(group):
                returned, partial_value = expert_rows(group[0].reshape(-1, D), group[1].reshape(-1, D), group[2].reshape(-1), group[3], group[4])
                return returned.reshape(blocks, CAP, D), partial_value

            returned, partials = lax.map(one_group, (send_in, send_grad, send_gate, proj_in[section_idx], proj_out[section_idx]))
            section_sum = section_sum + partials
            combined = jnp.einsum("btnc,nbcd->btd", placing, returned.astype(jnp.float32)).astype(jnp.bfloat16)
            micro_list.append(combined.reshape(TOKENS, D))
        section_grads.append(jnp.stack(micro_list))
        weight_grads.append(section_sum.astype(jnp.bfloat16))
    prev_grad = jnp.stack([section_grads[(section_idx + 1) % SECTIONS] for section_idx in range(SECTIONS)])
    return prev_grad, jnp.stack(weight_grads)
```

```python
import jax
import jax.numpy as jnp
from jax import lax
from jax.sharding import PartitionSpec as P

EXPERTS = 128
CAP = 24


def from_behind(value, axis, steps):
    count = lax.axis_size(axis)
    pairs = [(source, (source + steps) % count) for source in range(count)]
    return lax.ppermute(value, axis, pairs)


def build_slots(route_ids, gate_rows, groups, local_count):
    targets = jnp.arange(groups, dtype=jnp.int32) * local_count
    matches = route_ids[:, :, None] == targets
    routed = jnp.any(matches, axis=1)
    weight = jnp.sum(jnp.where(matches, gate_rows.astype(jnp.float32)[:, :, None], 0.0), axis=1)
    slot_rank = jnp.cumsum(routed.astype(jnp.int32), axis=0) - 1
    slot_ids = jnp.arange(CAP, dtype=jnp.int32)
    chosen = routed.T[:, None, :] & (slot_rank.T[:, None, :] == slot_ids[None, :, None])
    placing = chosen.astype(jnp.bfloat16)
    gated = jnp.where(chosen, weight.T[:, None, :], 0.0).astype(jnp.bfloat16)
    return (placing, gated)


def take_rows(placing, rows):
    return jnp.einsum("nct,td->ncd", placing, rows, preferred_element_type=jnp.float32).astype(
        jnp.bfloat16
    )


def expert_rows(rows_in, scaled, weight_in, weight_out):
    pre_act = jnp.dot(rows_in, weight_in, preferred_element_type=jnp.float32)
    sigmoid = jax.nn.sigmoid(pre_act)
    hidden = (pre_act * sigmoid).astype(jnp.bfloat16)
    hidden_grad = jnp.dot(scaled, weight_out.T, preferred_element_type=jnp.float32)
    pre_grad = (hidden_grad * sigmoid * (1.0 + pre_act * (1.0 - sigmoid))).astype(jnp.bfloat16)
    returned = jnp.dot(pre_grad, weight_in.T, preferred_element_type=jnp.float32).astype(
        jnp.bfloat16
    )
    return (returned, hidden)


def swap(value):
    return lax.all_to_all(value, "expert", split_axis=0, concat_axis=0, tiled=True)


def shards(inputs, upstream, routes, gate_weights, proj_in, proj_out):
    groups = lax.axis_size("expert")
    local_count = EXPERTS // groups
    micro_count = inputs.shape[1]
    width = inputs.shape[3]
    weight_in = proj_in[0, 0]
    weight_out = proj_out[0, 0]
    placings = []
    sends = []
    for micro in range(micro_count):
        placing, gated = build_slots(routes[0, micro], gate_weights[0, micro], groups, local_count)
        placings.append(placing)
        sends.append(
            jnp.concatenate(
                [take_rows(placing, inputs[0, micro]), take_rows(gated, upstream[0, micro])], axis=2
            )
        )
    received = [swap(send) for send in sends]
    returns = []
    hiddens = []
    scaleds = []
    for micro in range(micro_count):
        rows = received[micro].reshape(-1, 2 * width)
        scaled = rows[:, width:]
        returned, hidden = expert_rows(rows[:, :width], scaled, weight_in, weight_out)
        returns.append(swap(returned.reshape(groups, -1, width)))
        hiddens.append(hidden)
        scaleds.append(scaled)
    partial_value = sum(
        jnp.dot(hidden.T, scaled, preferred_element_type=jnp.float32)
        for hidden, scaled in zip(hiddens, scaleds)
    )
    other = from_behind(partial_value, "dp", 1)
    proj_grad = (partial_value + other).astype(jnp.bfloat16)[None, None]
    outputs = []
    for micro in range(micro_count):
        combined = jnp.einsum(
            "nct,ncd->td", placings[micro], returns[micro], preferred_element_type=jnp.float32
        ).astype(jnp.bfloat16)
        outputs.append(from_behind(combined, "pipe", -1))
    return (jnp.stack(outputs)[None], proj_grad)


def solution(mesh):
    placed = (
        P("pipe", None, ("expert", "dp"), None),
        P("pipe", None, ("expert", "dp"), None),
        P("pipe", None, ("expert", "dp"), None),
        P("pipe", None, ("expert", "dp"), None),
        P("pipe", "expert", None, None),
        P("pipe", "expert", None, None),
    )
    return jax.shard_map(
        shards,
        mesh=mesh,
        in_specs=placed,
        out_specs=(P("pipe", None, ("expert", "dp"), None), P("pipe", "expert", None, None)),
        check_vma=False,
    )
```

```python
import functools

import jax
import jax.numpy as jnp
from jax import lax
from jax.experimental import pallas as pl
from jax.experimental.pallas import tpu as pltpu
from jax.sharding import PartitionSpec as P

EXPERTS = 128
CAP = 24
COLUMNS = 2
AWAY = (0, 4, 1, 7, 2, 6, 3, 5)
EARLY = 4
MEANWHILE = (2, 3, 4, 5)
LAST = (0, 2, 3, 4, 5, 1, 6, 7)
BF16 = jnp.bfloat16
MIB = 1024 * 1024


def from_behind(value, axis, steps):
    count = lax.axis_size(axis)
    pairs = [(source, (source + steps) % count) for source in range(count)]
    return lax.ppermute(value, axis, pairs)


def swap_columns(value):
    return from_behind(value, "expert", lax.axis_size("expert") // COLUMNS)


def along_ring_behind(value, steps):
    sections, groups = lax.axis_size("pipe"), lax.axis_size("expert")
    ring = groups // COLUMNS
    pairs = [
        (s * groups + e, (s - 1) % sections * groups + e // ring * ring + (e + steps) % ring)
        for s in range(sections)
        for e in range(groups)
    ]
    return lax.ppermute(value, ("pipe", "expert"), pairs)


def along_ring(value, steps):
    groups = lax.axis_size("expert")
    ring = groups // COLUMNS
    pairs = [(e, e // ring * ring + (e + steps) % ring) for e in range(groups)]
    return lax.ppermute(value, "expert", pairs)


def together(held, blocks, positions):
    held, arrived = lax.optimization_barrier((held, [blocks[i] for i in positions]))
    return held, {**blocks, **dict(zip(positions, arrived))}


def build_slots(route_ids, gate_rows, experts):
    matches = route_ids[:, :, None] == experts
    routed = jnp.any(matches, axis=1)
    weight = jnp.sum(jnp.where(matches, gate_rows.astype(jnp.float32)[:, :, None], 0.0), axis=1)
    slot_rank = jnp.cumsum(routed.astype(jnp.int32), axis=0) - 1
    slot_ids = jnp.arange(CAP, dtype=jnp.int32)
    chosen = routed.T[:, None, :] & (slot_rank.T[:, None, :] == slot_ids[None, :, None])
    placing = chosen.astype(BF16)
    gated = jnp.where(chosen, weight.T[:, None, :], 0.0).astype(BF16)
    return jnp.stack([placing, gated]).reshape(2, experts.shape[0] * CAP, -1)


def take_rows(slots, inputs, upstream, micro, side_by_side):
    _, rows, tokens = slots.shape
    width = inputs.shape[3]
    blocks = rows // CAP
    piece = 512
    tile = width if side_by_side else width // 2
    tiles = width // tile

    def kernel(slots_ref, inputs_ref, upstream_ref, out_ref):
        def take(rows_ref):
            for start in range(0, tile, piece):
                taken = jnp.dot(
                    slots_ref[0],
                    rows_ref[0, 0, :, start : start + piece],
                    preferred_element_type=jnp.float32,
                )
                for n in range(blocks):
                    block = taken[n * CAP : (n + 1) * CAP].astype(BF16)
                    if side_by_side:
                        out_ref[:, n * width + start : n * width + start + piece] = block
                    else:
                        out_ref[n, :, start : start + piece] = block

        @pl.when(pl.program_id(0) < tiles)
        def _():
            take(inputs_ref)

        @pl.when(pl.program_id(0) >= tiles)
        def _():
            take(upstream_ref)

    if side_by_side:
        out_spec = pl.BlockSpec((CAP, blocks * width), lambda i: (0, i))
        out_shape = (CAP, 2 * blocks * width)
    else:
        out_spec = pl.BlockSpec((blocks, CAP, tile), lambda i: (0, 0, i))
        out_shape = (blocks, CAP, 2 * width)
    return pl.pallas_call(
        kernel,
        grid=(2 * tiles,),
        in_specs=[
            pl.BlockSpec((1, rows, tokens), lambda i: (i // tiles, 0, 0)),
            pl.BlockSpec((1, 1, tokens, tile), lambda i: (0, micro, 0, jnp.minimum(i, tiles - 1))),
            pl.BlockSpec((1, 1, tokens, tile), lambda i: (0, micro, 0, jnp.maximum(i - tiles, 0))),
        ],
        out_specs=out_spec,
        out_shape=pltpu.HBM(out_shape, BF16),
        cost_estimate=pl.CostEstimate(
            flops=4 * rows * tokens * width,
            bytes_accessed=4 * width * (rows + tokens),
            transcendentals=0,
        ),
        compiler_params=pltpu.CompilerParams(vmem_limit_bytes=24 * MIB),
    )(slots, inputs, upstream)


def pack(arrays, moves, out_widths, after=()):
    count, outs = len(arrays) + len(after), len(out_widths)

    def kernel(*refs):
        sources, targets = refs[:count], refs[count : count + outs]
        buffers, in_sems, out_sems = refs[count + outs : -2], refs[-2], refs[-1]
        reads = [
            pltpu.make_async_copy(
                sources[a].at[:, pl.ds(start, size)],
                buffers[o].at[:, pl.ds(to, size)],
                in_sems.at[n],
            )
            for n, (a, start, o, to, size) in enumerate(moves)
        ]
        writes = [
            pltpu.make_async_copy(buffers[o], targets[o], out_sems.at[o]) for o in range(outs)
        ]
        for read in reads:
            read.start()
        for o in range(outs):
            for read, move in zip(reads, moves):
                if move[2] == o:
                    read.wait()
            writes[o].start()
        for write in writes:
            write.wait()

    total = sum(out_widths) * CAP * 2
    shapes = [(CAP, size) for size in out_widths]
    return pl.pallas_call(
        kernel,
        in_specs=[pl.BlockSpec(memory_space=pl.ANY)] * count,
        out_specs=[pl.BlockSpec(memory_space=pl.ANY)] * outs,
        out_shape=[jax.ShapeDtypeStruct(shape, BF16) for shape in shapes],
        scratch_shapes=[pltpu.VMEM(shape, BF16) for shape in shapes]
        + [pltpu.SemaphoreType.DMA((len(moves),)), pltpu.SemaphoreType.DMA((outs,))],
        cost_estimate=pl.CostEstimate(flops=0, bytes_accessed=2 * total, transcendentals=0),
        compiler_params=pltpu.CompilerParams(vmem_limit_bytes=16 * MIB),
    )(*arrays, *after)


def pair_up(own, crossed, ring, after=()):
    size = own.shape[1] // ring
    moves = []
    for d in range(ring):
        moves.append((0, d * size, d, 0, size))
        moves.append((1, d * size, d, size, size))
    return pack([own, crossed], moves, [2 * size] * ring, after)


def expert_rows(blocks, me, weight_in, weight_out, after=()):
    width, hid = weight_in.shape
    one = not isinstance(blocks, list)
    arrays = [blocks] if one else blocks
    count = len(arrays)
    number = blocks.shape[0] if one else COLUMNS * count
    rows = number * CAP
    tile = 256
    piece = 512
    ring = number // COLUMNS

    def kernel(*refs):
        in_ref, out_ref, me_ref = refs[count : count + 3]
        backs = refs[count + 3 + len(after) :][:COLUMNS]
        mine, place = me_ref[0] // ring, me_ref[0] % ring
        hidden_ref, scaled_ref, stacked_ref, pre_grad_ref = refs[-4:]

        def block(n, column):
            columns = slice(column, column + piece)
            if one:
                source = (mine + n) % COLUMNS * ring + (place + ring - AWAY[n // COLUMNS]) % ring
                return refs[0][source, :, columns]
            shift = n % COLUMNS * 2 * width
            return refs[n // COLUMNS][:, column + shift : column + shift + piece]

        for n in range(0, number, 2):
            for target_ref, first in ((stacked_ref, 0), (scaled_ref, width)):
                for start in range(0, width, piece):
                    pair = [block(n + k, first + start).astype(jnp.float32) for k in range(2)]
                    target_ref[n * CAP : (n + 2) * CAP, start : start + piece] = jnp.concatenate(
                        pair, axis=0
                    ).astype(BF16)
        for start in range(0, hid, tile):
            pre_act = jnp.dot(
                stacked_ref[...],
                in_ref[:, start : start + tile],
                preferred_element_type=jnp.float32,
            )
            hidden_grad = lax.dot_general(
                scaled_ref[...],
                out_ref[start : start + tile, :],
                (((1,), (1,)), ((), ())),
                preferred_element_type=jnp.float32,
            )
            sigmoid = jax.nn.sigmoid(pre_act)
            hidden_ref[:, start : start + tile] = (pre_act * sigmoid).astype(BF16)
            pre_grad_ref[:, start : start + tile] = (
                hidden_grad * sigmoid * (1.0 + pre_act * (1.0 - sigmoid))
            ).astype(BF16)
        for start in range(0, width, tile):
            returned = lax.dot_general(
                pre_grad_ref[...],
                in_ref[start : start + tile, :],
                (((1,), (1,)), ((), ())),
                preferred_element_type=jnp.float32,
            )
            for n in range(number):
                rows_back = returned[n * CAP : (n + 1) * CAP].astype(BF16)
                to = n // COLUMNS * width + start
                backs[n % COLUMNS][:, to : to + tile] = rows_back

    shapes = [(CAP, ring * width)] * COLUMNS
    shapes = shapes + [(rows, hid), (rows, width)]
    return pl.pallas_call(
        kernel,
        in_specs=[pl.BlockSpec(memory_space=pltpu.VMEM)] * (count + 2)
        + [pl.BlockSpec(memory_space=pltpu.SMEM)]
        + [pl.BlockSpec(memory_space=pl.ANY)] * len(after),
        out_specs=[pl.BlockSpec(memory_space=pltpu.VMEM)] * len(shapes),
        out_shape=[jax.ShapeDtypeStruct(shape, BF16) for shape in shapes],
        scratch_shapes=[pltpu.VMEM((rows, width), BF16), pltpu.VMEM((rows, hid), BF16)],
        cost_estimate=pl.CostEstimate(
            flops=6 * rows * width * hid,
            bytes_accessed=2 * (rows * width * 4 + 2 * width * hid),
            transcendentals=rows * hid,
        ),
        compiler_params=pltpu.CompilerParams(vmem_limit_bytes=40 * MIB),
    )(*arrays, weight_in, weight_out, me.reshape(1), *after)


def combine(placing, arrived, after=()):
    rows, tokens = placing.shape
    count = len(arrived)
    width = arrived[0].shape[1] // COLUMNS
    piece = 512

    def kernel(placing_ref, *refs):
        out_ref = refs[-1]
        for start in range(0, width, piece):
            stacked = jnp.concatenate(
                [
                    refs[d][:, c * width + start : c * width + start + piece].astype(jnp.float32)
                    for c in range(COLUMNS)
                    for d in range(count)
                ],
                axis=0,
            )
            out_ref[:, start : start + piece] = lax.dot_general(
                placing_ref[...],
                stacked.astype(BF16),
                (((0,), (0,)), ((), ())),
                preferred_element_type=jnp.float32,
            ).astype(BF16)

    return pl.pallas_call(
        kernel,
        in_specs=[pl.BlockSpec(memory_space=pltpu.VMEM)] * (count + 1)
        + [pl.BlockSpec(memory_space=pl.ANY)] * len(after),
        out_specs=pl.BlockSpec(memory_space=pltpu.VMEM),
        out_shape=jax.ShapeDtypeStruct((tokens, width), BF16),
        cost_estimate=pl.CostEstimate(
            flops=2 * rows * tokens * width,
            bytes_accessed=2 * (rows + tokens) * width,
            transcendentals=0,
        ),
        compiler_params=pltpu.CompilerParams(vmem_limit_bytes=24 * MIB),
    )(placing, *arrived, *after)


def weight_grad(hiddens, scaleds, after):
    rows, hid = hiddens[0].shape
    width = scaleds[0].shape[1]
    count = len(hiddens)
    tile = 512

    def kernel(*refs):
        out_ref = refs[-1]
        for start in range(0, hid, 256):
            total = None
            for hidden_ref, scaled_ref in zip(refs[:count], refs[count : 2 * count]):
                term = lax.dot_general(
                    hidden_ref[:, start : start + 256],
                    scaled_ref[...],
                    (((0,), (0,)), ((), ())),
                    preferred_element_type=jnp.float32,
                )
                total = term if total is None else total + term
            out_ref[start : start + 256, :] = total

    return pl.pallas_call(
        kernel,
        grid=(width // tile,),
        in_specs=[pl.BlockSpec((rows, hid), lambda i: (0, 0))] * count
        + [pl.BlockSpec((rows, tile), lambda i: (0, i))] * count
        + [pl.BlockSpec(memory_space=pl.ANY)] * len(after),
        out_specs=pl.BlockSpec((hid, tile), lambda i: (0, i)),
        out_shape=jax.ShapeDtypeStruct((hid, width), jnp.float32),
        cost_estimate=pl.CostEstimate(
            flops=2 * count * rows * hid * width,
            bytes_accessed=4 * hid * width + 2 * count * rows * (hid + width),
            transcendentals=0,
        ),
        compiler_params=pltpu.CompilerParams(vmem_limit_bytes=24 * MIB),
    )(*hiddens, *scaleds, *after)


def swap_groups(value):
    return lax.all_to_all(value, "expert", split_axis=0, concat_axis=0, tiled=True)


def shards(inputs, upstream, routes, gate_weights, proj_in, proj_out):
    groups = lax.axis_size("expert")
    ring = groups // COLUMNS
    local_count = EXPERTS // groups
    width = inputs.shape[3]
    weight_in = proj_in[0, 0]
    weight_out = proj_out[0, 0]
    me = lax.axis_index("expert")
    order = jnp.arange(groups, dtype=jnp.int32)
    place = (jnp.array(AWAY * COLUMNS, jnp.int32) + me) % ring
    near = (order // ring + me // ring) % COLUMNS * ring + place

    slots_0 = build_slots(routes[0, 0], gate_weights[0, 0], order * local_count)
    first = swap_groups(take_rows(slots_0, inputs, upstream, 0, False))

    slots_1 = build_slots(routes[0, 1], gate_weights[0, 1], near * local_count)
    behind = from_behind(slots_1[0], "pipe", -1)
    own_rows, away_rows = slots_1[:, : ring * CAP], slots_1[:, ring * CAP :]

    def send_pack(start, stop):
        count = stop - start
        rows = slice(start * CAP, stop * CAP)
        away = swap_columns(take_rows(away_rows[:, rows], inputs, upstream, 1, True))
        own = take_rows(own_rows[:, rows], inputs, upstream, 1, True)
        moves = []
        for n in range(count):
            for c in range(COLUMNS):
                for part in range(2):
                    column = (part * count + n) * width
                    moves.append((c, column, n, (c * 2 + part) * width, width))
        return pack([own, away], moves, [4 * width] * count)

    blocks = send_pack(0, EARLY)
    second = {i: along_ring(blocks[i], AWAY[i]) for i in range(1, EARLY)}
    own_0, away_0, hidden_0, scaled_0 = expert_rows(first, me, weight_in, weight_out)
    (own_0, away_0, behind), second = together((own_0, away_0, behind), second, range(1, EARLY))
    blocks += send_pack(EARLY, ring)
    second[0] = blocks[0]
    second.update({i: along_ring(blocks[i], AWAY[i]) for i in range(EARLY, ring)})
    back = pair_up(own_0, swap_columns(away_0), ring)
    rest = [i for i in range(1, ring) if i not in MEANWHILE]

    own_1, away_1, hidden_1, scaled_1 = expert_rows(
        [second[i] for i in range(ring)], me, weight_in, weight_out, back[:1]
    )
    back_0 = {i: along_ring(back[i], -AWAY[i]) for i in MEANWHILE}
    partial_value = weight_grad([hidden_0, hidden_1], [scaled_0, scaled_1], [])
    held = (own_1, away_1, partial_value, [back[i] for i in rest])
    (own_1, away_1, partial_value, held), back_0 = together(held, back_0, MEANWHILE)
    back_0.update({i: along_ring(held[n], -AWAY[i]) for n, i in enumerate(rest)})
    back_0[0] = back[0]
    proj_grad = (partial_value + from_behind(partial_value, "dp", 1)).astype(BF16)
    after = [proj_grad] + [back_0[i] for i in rest]
    back = pair_up(own_1, swap_columns(away_1), ring, after)
    back_1 = [along_ring_behind(back[i], -AWAY[i]) for i in LAST]
    back_1 = [back_1[LAST.index(i)] for i in range(ring)]

    placing = jnp.take(slots_0[0].reshape(groups, CAP, -1), near, axis=0).reshape(groups * CAP, -1)
    grad_0 = from_behind(combine(placing, [back_0[i] for i in range(ring)]), "pipe", -1)
    grad_1 = combine(behind, back_1, [grad_0])
    return (jnp.stack([grad_0, grad_1])[None], proj_grad[None, None])


def solution(mesh):
    placed = (
        P("pipe", None, ("expert", "dp"), None),
        P("pipe", None, ("expert", "dp"), None),
        P("pipe", None, ("expert", "dp"), None),
        P("pipe", None, ("expert", "dp"), None),
        P("pipe", "expert", None, None),
        P("pipe", "expert", None, None),
    )
    return jax.shard_map(
        shards,
        mesh=mesh,
        in_specs=placed,
        out_specs=(P("pipe", None, ("expert", "dp"), None), P("pipe", "expert", None, None)),
        check_vma=False,
    )
```

```python
import functools

import jax
import jax.numpy as jnp
from jax import lax
from jax.experimental import pallas as pl
from jax.experimental.pallas import tpu as pltpu
from jax.sharding import PartitionSpec as P

EXPERTS = 128
CAP = 24
COLUMNS = 2
AWAY = (0, 4, 1, 7, 2, 6, 3, 5)
EARLY = 4
MEANWHILE = (2, 3, 4, 5)
LAST = (2, 3, 0, 4, 5, 1, 6, 7)
BF16 = jnp.bfloat16
MIB = 1024 * 1024


def from_behind(value, axis, steps):
    count = lax.axis_size(axis)
    pairs = [(source, (source + steps) % count) for source in range(count)]
    return lax.ppermute(value, axis, pairs)


def swap_columns(value):
    return from_behind(value, "expert", lax.axis_size("expert") // COLUMNS)


def along_ring_behind(value, steps):
    sections, groups = lax.axis_size("pipe"), lax.axis_size("expert")
    ring = groups // COLUMNS
    pairs = [
        (s * groups + e, (s - 1) % sections * groups + e // ring * ring + (e + steps) % ring)
        for s in range(sections)
        for e in range(groups)
    ]
    return lax.ppermute(value, ("pipe", "expert"), pairs)


def along_ring(value, steps):
    groups = lax.axis_size("expert")
    ring = groups // COLUMNS
    pairs = [(e, e // ring * ring + (e + steps) % ring) for e in range(groups)]
    return lax.ppermute(value, "expert", pairs)


def together(held, blocks, positions):
    held, arrived = lax.optimization_barrier((held, [blocks[i] for i in positions]))
    return held, {**blocks, **dict(zip(positions, arrived))}


def build_slots(route_ids, gate_rows, experts):
    matches = route_ids[:, :, None] == experts
    routed = jnp.any(matches, axis=1)
    weight = jnp.sum(jnp.where(matches, gate_rows.astype(jnp.float32)[:, :, None], 0.0), axis=1)
    slot_rank = jnp.cumsum(routed.astype(jnp.int32), axis=0) - 1
    slot_ids = jnp.arange(CAP, dtype=jnp.int32)
    chosen = routed.T[:, None, :] & (slot_rank.T[:, None, :] == slot_ids[None, :, None])
    placing = chosen.astype(BF16)
    gated = jnp.where(chosen, weight.T[:, None, :], 0.0).astype(BF16)
    return jnp.stack([placing, gated]).reshape(2, experts.shape[0] * CAP, -1)


def take_rows(slots, inputs, upstream, micro, side_by_side):
    _, rows, tokens = slots.shape
    width = inputs.shape[3]
    blocks = rows // CAP
    piece = 512
    tile = width if side_by_side else width // 2
    tiles = width // tile

    def kernel(slots_ref, inputs_ref, upstream_ref, out_ref):
        def take(rows_ref):
            for start in range(0, tile, piece):
                taken = jnp.dot(
                    slots_ref[0],
                    rows_ref[0, 0, :, start : start + piece],
                    preferred_element_type=jnp.float32,
                )
                for n in range(blocks):
                    block = taken[n * CAP : (n + 1) * CAP].astype(BF16)
                    if side_by_side:
                        out_ref[:, n * width + start : n * width + start + piece] = block
                    else:
                        out_ref[n, :, start : start + piece] = block

        @pl.when(pl.program_id(0) < tiles)
        def _():
            take(inputs_ref)

        @pl.when(pl.program_id(0) >= tiles)
        def _():
            take(upstream_ref)

    if side_by_side:
        out_spec = pl.BlockSpec((CAP, blocks * width), lambda i: (0, i))
        out_shape = (CAP, 2 * blocks * width)
    else:
        out_spec = pl.BlockSpec((blocks, CAP, tile), lambda i: (0, 0, i))
        out_shape = (blocks, CAP, 2 * width)
    return pl.pallas_call(
        kernel,
        grid=(2 * tiles,),
        in_specs=[
            pl.BlockSpec((1, rows, tokens), lambda i: (i // tiles, 0, 0)),
            pl.BlockSpec((1, 1, tokens, tile), lambda i: (0, micro, 0, jnp.minimum(i, tiles - 1))),
            pl.BlockSpec((1, 1, tokens, tile), lambda i: (0, micro, 0, jnp.maximum(i - tiles, 0))),
        ],
        out_specs=out_spec,
        out_shape=pltpu.HBM(out_shape, BF16),
        cost_estimate=pl.CostEstimate(
            flops=4 * rows * tokens * width,
            bytes_accessed=4 * width * (rows + tokens),
            transcendentals=0,
        ),
        compiler_params=pltpu.CompilerParams(vmem_limit_bytes=24 * MIB),
    )(slots, inputs, upstream)


def pack(arrays, moves, out_widths, after=()):
    count, outs = len(arrays) + len(after), len(out_widths)

    def kernel(*refs):
        sources, targets = refs[:count], refs[count : count + outs]
        buffers, in_sems, out_sems = refs[count + outs : -2], refs[-2], refs[-1]
        reads = [
            pltpu.make_async_copy(
                sources[a].at[:, pl.ds(start, size)],
                buffers[o].at[:, pl.ds(to, size)],
                in_sems.at[n],
            )
            for n, (a, start, o, to, size) in enumerate(moves)
        ]
        writes = [
            pltpu.make_async_copy(buffers[o], targets[o], out_sems.at[o]) for o in range(outs)
        ]
        for read in reads:
            read.start()
        for o in range(outs):
            for read, move in zip(reads, moves):
                if move[2] == o:
                    read.wait()
            writes[o].start()
        for write in writes:
            write.wait()

    total = sum(out_widths) * CAP * 2
    shapes = [(CAP, size) for size in out_widths]
    return pl.pallas_call(
        kernel,
        in_specs=[pl.BlockSpec(memory_space=pl.ANY)] * count,
        out_specs=[pl.BlockSpec(memory_space=pl.ANY)] * outs,
        out_shape=[jax.ShapeDtypeStruct(shape, BF16) for shape in shapes],
        scratch_shapes=[pltpu.VMEM(shape, BF16) for shape in shapes]
        + [pltpu.SemaphoreType.DMA((len(moves),)), pltpu.SemaphoreType.DMA((outs,))],
        cost_estimate=pl.CostEstimate(flops=0, bytes_accessed=2 * total, transcendentals=0),
        compiler_params=pltpu.CompilerParams(vmem_limit_bytes=16 * MIB),
    )(*arrays, *after)


def pair_up(own, crossed, ring, after=()):
    size = own.shape[1] // ring
    moves = []
    for d in range(ring):
        moves.append((0, d * size, d, 0, size))
        moves.append((1, d * size, d, size, size))
    return pack([own, crossed], moves, [2 * size] * ring, after)


def expert_rows(blocks, me, weight_in, weight_out, after=()):
    width, hid = weight_in.shape
    one = not isinstance(blocks, list)
    arrays = [blocks] if one else blocks
    count = len(arrays)
    number = blocks.shape[0] if one else COLUMNS * count
    rows = number * CAP
    tile = 256
    piece = 512
    ring = number // COLUMNS

    def kernel(*refs):
        in_ref, out_ref, me_ref = refs[count : count + 3]
        backs = refs[count + 3 + len(after) :][:COLUMNS]
        mine, place = me_ref[0] // ring, me_ref[0] % ring
        hidden_ref, scaled_ref, stacked_ref, pre_grad_ref = refs[-4:]

        def block(n, column):
            columns = slice(column, column + piece)
            if one:
                source = (mine + n) % COLUMNS * ring + (place + ring - AWAY[n // COLUMNS]) % ring
                return refs[0][source, :, columns]
            shift = n % COLUMNS * 2 * width
            return refs[n // COLUMNS][:, column + shift : column + shift + piece]

        for n in range(0, number, 2):
            for target_ref, first in ((stacked_ref, 0), (scaled_ref, width)):
                for start in range(0, width, piece):
                    pair = [block(n + k, first + start).astype(jnp.float32) for k in range(2)]
                    target_ref[n * CAP : (n + 2) * CAP, start : start + piece] = jnp.concatenate(
                        pair, axis=0
                    ).astype(BF16)
        for start in range(0, hid, tile):
            pre_act = jnp.dot(
                stacked_ref[...],
                in_ref[:, start : start + tile],
                preferred_element_type=jnp.float32,
            )
            hidden_grad = lax.dot_general(
                scaled_ref[...],
                out_ref[start : start + tile, :],
                (((1,), (1,)), ((), ())),
                preferred_element_type=jnp.float32,
            )
            sigmoid = jax.nn.sigmoid(pre_act)
            hidden_ref[:, start : start + tile] = (pre_act * sigmoid).astype(BF16)
            pre_grad_ref[:, start : start + tile] = (
                hidden_grad * sigmoid * (1.0 + pre_act * (1.0 - sigmoid))
            ).astype(BF16)
        for start in range(0, width, tile):
            returned = lax.dot_general(
                pre_grad_ref[...],
                in_ref[start : start + tile, :],
                (((1,), (1,)), ((), ())),
                preferred_element_type=jnp.float32,
            )
            for n in range(number):
                rows_back = returned[n * CAP : (n + 1) * CAP].astype(BF16)
                to = n // COLUMNS * width + start
                backs[n % COLUMNS][:, to : to + tile] = rows_back

    shapes = [(CAP, ring * width)] * COLUMNS
    shapes = shapes + [(rows, hid), (rows, width)]
    return pl.pallas_call(
        kernel,
        in_specs=[pl.BlockSpec(memory_space=pltpu.VMEM)] * (count + 2)
        + [pl.BlockSpec(memory_space=pltpu.SMEM)]
        + [pl.BlockSpec(memory_space=pl.ANY)] * len(after),
        out_specs=[pl.BlockSpec(memory_space=pltpu.VMEM)] * len(shapes),
        out_shape=[jax.ShapeDtypeStruct(shape, BF16) for shape in shapes],
        scratch_shapes=[pltpu.VMEM((rows, width), BF16), pltpu.VMEM((rows, hid), BF16)],
        cost_estimate=pl.CostEstimate(
            flops=6 * rows * width * hid,
            bytes_accessed=2 * (rows * width * 4 + 2 * width * hid),
            transcendentals=rows * hid,
        ),
        compiler_params=pltpu.CompilerParams(vmem_limit_bytes=40 * MIB),
    )(*arrays, weight_in, weight_out, me.reshape(1), *after)


def combine(placing, arrived, after=()):
    rows, tokens = placing.shape
    count = len(arrived)
    width = arrived[0].shape[1] // COLUMNS
    piece = 512

    def kernel(placing_ref, *refs):
        out_ref = refs[-1]
        for start in range(0, width, piece):
            stacked = jnp.concatenate(
                [
                    refs[d][:, c * width + start : c * width + start + piece].astype(jnp.float32)
                    for c in range(COLUMNS)
                    for d in range(count)
                ],
                axis=0,
            )
            out_ref[:, start : start + piece] = lax.dot_general(
                placing_ref[...],
                stacked.astype(BF16),
                (((0,), (0,)), ((), ())),
                preferred_element_type=jnp.float32,
            ).astype(BF16)

    return pl.pallas_call(
        kernel,
        in_specs=[pl.BlockSpec(memory_space=pltpu.VMEM)] * (count + 1)
        + [pl.BlockSpec(memory_space=pl.ANY)] * len(after),
        out_specs=pl.BlockSpec(memory_space=pltpu.VMEM),
        out_shape=jax.ShapeDtypeStruct((tokens, width), BF16),
        cost_estimate=pl.CostEstimate(
            flops=2 * rows * tokens * width,
            bytes_accessed=2 * (rows + tokens) * width,
            transcendentals=0,
        ),
        compiler_params=pltpu.CompilerParams(vmem_limit_bytes=24 * MIB),
    )(placing, *arrived, *after)


def weight_grad(hiddens, scaleds, after):
    rows, hid = hiddens[0].shape
    width = scaleds[0].shape[1]
    count = len(hiddens)
    tile = 512

    def kernel(*refs):
        out_ref = refs[-1]
        for start in range(0, hid, 256):
            total = None
            for hidden_ref, scaled_ref in zip(refs[:count], refs[count : 2 * count]):
                term = lax.dot_general(
                    hidden_ref[:, start : start + 256],
                    scaled_ref[...],
                    (((0,), (0,)), ((), ())),
                    preferred_element_type=jnp.float32,
                )
                total = term if total is None else total + term
            out_ref[start : start + 256, :] = total

    return pl.pallas_call(
        kernel,
        grid=(width // tile,),
        in_specs=[pl.BlockSpec((rows, hid), lambda i: (0, 0))] * count
        + [pl.BlockSpec((rows, tile), lambda i: (0, i))] * count
        + [pl.BlockSpec(memory_space=pl.ANY)] * len(after),
        out_specs=pl.BlockSpec((hid, tile), lambda i: (0, i)),
        out_shape=jax.ShapeDtypeStruct((hid, width), jnp.float32),
        cost_estimate=pl.CostEstimate(
            flops=2 * count * rows * hid * width,
            bytes_accessed=4 * hid * width + 2 * count * rows * (hid + width),
            transcendentals=0,
        ),
        compiler_params=pltpu.CompilerParams(vmem_limit_bytes=24 * MIB),
    )(*hiddens, *scaleds, *after)


def swap_groups(value):
    return lax.all_to_all(value, "expert", split_axis=0, concat_axis=0, tiled=True)


def shards(inputs, upstream, routes, gate_weights, proj_in, proj_out):
    groups = lax.axis_size("expert")
    ring = groups // COLUMNS
    local_count = EXPERTS // groups
    width = inputs.shape[3]
    weight_in = proj_in[0, 0]
    weight_out = proj_out[0, 0]
    me = lax.axis_index("expert")
    order = jnp.arange(groups, dtype=jnp.int32)
    place = (jnp.array(AWAY * COLUMNS, jnp.int32) + me) % ring
    near = (order // ring + me // ring) % COLUMNS * ring + place

    slots_0 = build_slots(routes[0, 0], gate_weights[0, 0], order * local_count)
    first = swap_groups(take_rows(slots_0, inputs, upstream, 0, False))

    slots_1 = build_slots(routes[0, 1], gate_weights[0, 1], near * local_count)
    behind = from_behind(slots_1[0], "pipe", -1)
    own_rows, away_rows = slots_1[:, : ring * CAP], slots_1[:, ring * CAP :]

    def send_pack(start, stop):
        count = stop - start
        rows = slice(start * CAP, stop * CAP)
        away = swap_columns(take_rows(away_rows[:, rows], inputs, upstream, 1, True))
        own = take_rows(own_rows[:, rows], inputs, upstream, 1, True)
        moves = []
        for n in range(count):
            for c in range(COLUMNS):
                for part in range(2):
                    column = (part * count + n) * width
                    moves.append((c, column, n, (c * 2 + part) * width, width))
        return pack([own, away], moves, [4 * width] * count)

    blocks = send_pack(0, EARLY)
    second = {i: along_ring(blocks[i], AWAY[i]) for i in range(1, EARLY)}
    own_0, away_0, hidden_0, scaled_0 = expert_rows(first, me, weight_in, weight_out)
    held = (own_0, away_0, behind, send_pack(EARLY, ring))
    (own_0, away_0, behind, late), second = together(held, second, range(1, EARLY))
    blocks += late
    second[0] = blocks[0]
    second.update({i: along_ring(blocks[i], AWAY[i]) for i in range(EARLY, ring)})
    back = pair_up(own_0, swap_columns(away_0), ring)
    rest = [i for i in range(1, ring) if i not in MEANWHILE]

    own_1, away_1, hidden_1, scaled_1 = expert_rows(
        [second[i] for i in range(ring)], me, weight_in, weight_out, back[:1]
    )
    back_0 = {i: along_ring(back[i], -AWAY[i]) for i in MEANWHILE}
    partial_value = weight_grad([hidden_0, hidden_1], [scaled_0, scaled_1], [])
    held = (own_1, away_1, partial_value, [back[i] for i in rest])
    (own_1, away_1, partial_value, held), back_0 = together(held, back_0, MEANWHILE)
    back_0.update({i: along_ring(held[n], -AWAY[i]) for n, i in enumerate(rest)})
    back_0[0] = back[0]
    held = (partial_value, swap_columns(away_1))
    (partial_value, away_1), back_0 = together(held, back_0, rest)
    back = pair_up(own_1, away_1, ring)
    proj_grad = (partial_value + from_behind(partial_value, "dp", 1)).astype(BF16)
    back_1 = [along_ring_behind(back[i], -AWAY[i]) for i in LAST]
    back_1 = [back_1[LAST.index(i)] for i in range(ring)]

    placing = jnp.take(slots_0[0].reshape(groups, CAP, -1), near, axis=0).reshape(groups * CAP, -1)
    grad_0 = from_behind(combine(placing, [back_0[i] for i in range(ring)]), "pipe", -1)
    grad_1 = combine(behind, back_1, [grad_0, proj_grad])
    return (jnp.stack([grad_0, grad_1])[None], proj_grad[None, None])


def solution(mesh):
    placed = (
        P("pipe", None, ("expert", "dp"), None),
        P("pipe", None, ("expert", "dp"), None),
        P("pipe", None, ("expert", "dp"), None),
        P("pipe", None, ("expert", "dp"), None),
        P("pipe", "expert", None, None),
        P("pipe", "expert", None, None),
    )
    return jax.shard_map(
        shards,
        mesh=mesh,
        in_specs=placed,
        out_specs=(P("pipe", None, ("expert", "dp"), None), P("pipe", "expert", None, None)),
        check_vma=False,
    )
```

```python
import functools

import jax
import jax.numpy as jnp
from jax import lax
from jax.experimental import pallas as pl
from jax.experimental.pallas import tpu as pltpu
from jax.sharding import PartitionSpec as P

EXPERTS = 128
CAP = 24
COLUMNS = 2
AWAY = (0, 4, 1, 7, 2, 6, 3, 5)
EARLY = 4
MEANWHILE = (2, 3, 4, 5)
LAST = (6, 7, 4, 5, 0, 1, 2, 3)
BF16 = jnp.bfloat16
MIB = 1024 * 1024


def from_behind(value, axis, steps):
    count = lax.axis_size(axis)
    pairs = [(source, (source + steps) % count) for source in range(count)]
    return lax.ppermute(value, axis, pairs)


def swap_columns(value):
    return from_behind(value, "expert", lax.axis_size("expert") // COLUMNS)


def along_ring_behind(value, steps):
    sections, groups = lax.axis_size("pipe"), lax.axis_size("expert")
    ring = groups // COLUMNS
    pairs = [
        (s * groups + e, (s - 1) % sections * groups + e // ring * ring + (e + steps) % ring)
        for s in range(sections)
        for e in range(groups)
    ]
    return lax.ppermute(value, ("pipe", "expert"), pairs)


def along_ring(value, steps):
    groups = lax.axis_size("expert")
    ring = groups // COLUMNS
    pairs = [(e, e // ring * ring + (e + steps) % ring) for e in range(groups)]
    return lax.ppermute(value, "expert", pairs)


def together(held, blocks, positions):
    held, arrived = lax.optimization_barrier((held, [blocks[i] for i in positions]))
    return held, {**blocks, **dict(zip(positions, arrived))}


def build_slots(route_ids, gate_rows, experts):
    matches = route_ids[:, :, None] == experts
    routed = jnp.any(matches, axis=1)
    weight = jnp.sum(jnp.where(matches, gate_rows.astype(jnp.float32)[:, :, None], 0.0), axis=1)
    slot_rank = jnp.cumsum(routed.astype(jnp.int32), axis=0) - 1
    slot_ids = jnp.arange(CAP, dtype=jnp.int32)
    chosen = routed.T[:, None, :] & (slot_rank.T[:, None, :] == slot_ids[None, :, None])
    placing = chosen.astype(BF16)
    gated = jnp.where(chosen, weight.T[:, None, :], 0.0).astype(BF16)
    return jnp.stack([placing, gated]).reshape(2, experts.shape[0] * CAP, -1)


def take_rows(slots, inputs, upstream, micro, side_by_side):
    _, rows, tokens = slots.shape
    width = inputs.shape[3]
    blocks = rows // CAP
    piece = 512
    tile = width if side_by_side else width // 2
    tiles = width // tile

    def kernel(slots_ref, inputs_ref, upstream_ref, out_ref):
        def take(rows_ref):
            for start in range(0, tile, piece):
                taken = jnp.dot(
                    slots_ref[0],
                    rows_ref[0, 0, :, start : start + piece],
                    preferred_element_type=jnp.float32,
                )
                for n in range(blocks):
                    block = taken[n * CAP : (n + 1) * CAP].astype(BF16)
                    if side_by_side:
                        out_ref[:, n * width + start : n * width + start + piece] = block
                    else:
                        out_ref[n, :, start : start + piece] = block

        @pl.when(pl.program_id(0) < tiles)
        def _():
            take(inputs_ref)

        @pl.when(pl.program_id(0) >= tiles)
        def _():
            take(upstream_ref)

    if side_by_side:
        out_spec = pl.BlockSpec((CAP, blocks * width), lambda i: (0, i))
        out_shape = (CAP, 2 * blocks * width)
    else:
        out_spec = pl.BlockSpec((blocks, CAP, tile), lambda i: (0, 0, i))
        out_shape = (blocks, CAP, 2 * width)
    return pl.pallas_call(
        kernel,
        grid=(2 * tiles,),
        in_specs=[
            pl.BlockSpec((1, rows, tokens), lambda i: (i // tiles, 0, 0)),
            pl.BlockSpec((1, 1, tokens, tile), lambda i: (0, micro, 0, jnp.minimum(i, tiles - 1))),
            pl.BlockSpec((1, 1, tokens, tile), lambda i: (0, micro, 0, jnp.maximum(i - tiles, 0))),
        ],
        out_specs=out_spec,
        out_shape=pltpu.HBM(out_shape, BF16),
        cost_estimate=pl.CostEstimate(
            flops=4 * rows * tokens * width,
            bytes_accessed=4 * width * (rows + tokens),
            transcendentals=0,
        ),
        compiler_params=pltpu.CompilerParams(vmem_limit_bytes=24 * MIB),
    )(slots, inputs, upstream)


def route_and_take(routes, gate_weights, inputs, upstream, micro, groups, local_count):
    tokens, width = inputs.shape[2:]
    top = routes.shape[3]
    rows = groups * CAP
    piece = 512
    tile = width // 2
    tiles = width // tile

    def kernel(routes_ref, gate_ref, inputs_ref, upstream_ref, out_ref, slots_ref):
        @pl.when(pl.program_id(0) == 0)
        def _():
            experts = routes_ref[0, 0].astype(jnp.float32)
            gates = gate_ref[0, 0].astype(jnp.float32)
            targets = lax.broadcasted_iota(jnp.int32, (groups, tokens), 0) * local_count
            targets = targets.astype(jnp.float32)
            routed = jnp.zeros((groups, tokens), jnp.float32)
            weight = jnp.zeros((groups, tokens), jnp.float32)
            for k in range(top):
                match = experts[k : k + 1] == targets
                routed = jnp.where(match, 1.0, routed)
                weight = weight + jnp.where(match, gates[k : k + 1], 0.0)
            upto = jnp.where(
                lax.broadcasted_iota(jnp.int32, (tokens, tokens), 0)
                <= lax.broadcasted_iota(jnp.int32, (tokens, tokens), 1),
                1.0,
                0.0,
            ).astype(BF16)
            rank = jnp.dot(routed.astype(BF16), upto, preferred_element_type=jnp.float32)
            slot = jnp.where(routed > 0.5, rank, 0.0)
            ids = lax.broadcasted_iota(jnp.int32, (CAP, tokens), 0).astype(jnp.float32) + 1.0
            for n in range(0, groups, 2):
                chosen = [slot[n + k : n + k + 1] == ids for k in range(2)]
                ones = [jnp.where(pick, 1.0, 0.0) for pick in chosen]
                gated = [
                    jnp.where(pick, weight[n + k : n + k + 1], 0.0) for k, pick in enumerate(chosen)
                ]
                at = slice(n * CAP, (n + 2) * CAP)
                slots_ref[0, at, :] = jnp.concatenate(ones, axis=0).astype(BF16)
                slots_ref[1, at, :] = jnp.concatenate(gated, axis=0).astype(BF16)

        def take(which, rows_ref):
            for start in range(0, tile, piece):
                taken = jnp.dot(
                    slots_ref[which],
                    rows_ref[0, 0, :, start : start + piece],
                    preferred_element_type=jnp.float32,
                )
                for n in range(groups):
                    block = taken[n * CAP : (n + 1) * CAP].astype(BF16)
                    out_ref[n, :, start : start + piece] = block

        @pl.when(pl.program_id(0) < tiles)
        def _():
            take(0, inputs_ref)

        @pl.when(pl.program_id(0) >= tiles)
        def _():
            take(1, upstream_ref)

    return pl.pallas_call(
        kernel,
        grid=(2 * tiles,),
        in_specs=[
            pl.BlockSpec((1, 1, top, tokens), lambda i: (0, micro, 0, 0)),
            pl.BlockSpec((1, 1, top, tokens), lambda i: (0, micro, 0, 0)),
            pl.BlockSpec((1, 1, tokens, tile), lambda i: (0, micro, 0, jnp.minimum(i, tiles - 1))),
            pl.BlockSpec((1, 1, tokens, tile), lambda i: (0, micro, 0, jnp.maximum(i - tiles, 0))),
        ],
        out_specs=pl.BlockSpec((groups, CAP, tile), lambda i: (0, 0, i)),
        out_shape=pltpu.HBM((groups, CAP, 2 * width), BF16),
        scratch_shapes=[pltpu.VMEM((2, rows, tokens), BF16)],
        cost_estimate=pl.CostEstimate(
            flops=4 * rows * tokens * width,
            bytes_accessed=4 * width * (rows + tokens),
            transcendentals=0,
        ),
        compiler_params=pltpu.CompilerParams(vmem_limit_bytes=24 * MIB),
    )(
        jnp.swapaxes(routes, 2, 3),
        jnp.swapaxes(gate_weights, 2, 3),
        pltpu.with_memory_space_constraint(inputs, pltpu.HBM),
        pltpu.with_memory_space_constraint(upstream, pltpu.HBM),
    )


def pack(arrays, moves, out_widths, after=()):
    count, outs = len(arrays) + len(after), len(out_widths)

    def kernel(*refs):
        sources, targets = refs[:count], refs[count : count + outs]
        buffers, in_sems, out_sems = refs[count + outs : -2], refs[-2], refs[-1]
        reads = [
            pltpu.make_async_copy(
                sources[a].at[:, pl.ds(start, size)],
                buffers[o].at[:, pl.ds(to, size)],
                in_sems.at[n],
            )
            for n, (a, start, o, to, size) in enumerate(moves)
        ]
        writes = [
            pltpu.make_async_copy(buffers[o], targets[o], out_sems.at[o]) for o in range(outs)
        ]
        for read in reads:
            read.start()
        for o in range(outs):
            for read, move in zip(reads, moves):
                if move[2] == o:
                    read.wait()
            writes[o].start()
        for write in writes:
            write.wait()

    total = sum(out_widths) * CAP * 2
    shapes = [(CAP, size) for size in out_widths]
    return pl.pallas_call(
        kernel,
        in_specs=[pl.BlockSpec(memory_space=pl.ANY)] * count,
        out_specs=[pl.BlockSpec(memory_space=pl.ANY)] * outs,
        out_shape=[jax.ShapeDtypeStruct(shape, BF16) for shape in shapes],
        scratch_shapes=[pltpu.VMEM(shape, BF16) for shape in shapes]
        + [pltpu.SemaphoreType.DMA((len(moves),)), pltpu.SemaphoreType.DMA((outs,))],
        cost_estimate=pl.CostEstimate(flops=0, bytes_accessed=2 * total, transcendentals=0),
        compiler_params=pltpu.CompilerParams(vmem_limit_bytes=16 * MIB),
    )(*arrays, *after)


def pair_up(own, crossed, ring, after=()):
    size = own.shape[1] // ring
    moves = []
    for d in range(ring):
        moves.append((0, d * size, d, 0, size))
        moves.append((1, d * size, d, size, size))
    return pack([own, crossed], moves, [2 * size] * ring, after)


def expert_rows(blocks, me, weight_in, weight_out, after=()):
    width, hid = weight_in.shape
    one = not isinstance(blocks, list)
    arrays = [blocks] if one else blocks
    count = len(arrays)
    number = blocks.shape[0] if one else COLUMNS * count
    rows = number * CAP
    tile = 256
    piece = 512
    ring = number // COLUMNS

    def kernel(*refs):
        in_ref, out_ref, me_ref = refs[count : count + 3]
        backs = refs[count + 3 + len(after) :][:COLUMNS]
        mine, place = me_ref[0] // ring, me_ref[0] % ring
        hidden_ref, scaled_ref, stacked_ref, pre_grad_ref = refs[-4:]

        def block(n, column):
            columns = slice(column, column + piece)
            if one:
                source = (mine + n) % COLUMNS * ring + (place + ring - AWAY[n // COLUMNS]) % ring
                return refs[0][source, :, columns]
            shift = n % COLUMNS * 2 * width
            return refs[n // COLUMNS][:, column + shift : column + shift + piece]

        for n in range(0, number, 2):
            for target_ref, first in ((stacked_ref, 0), (scaled_ref, width)):
                for start in range(0, width, piece):
                    pair = [block(n + k, first + start).astype(jnp.float32) for k in range(2)]
                    target_ref[n * CAP : (n + 2) * CAP, start : start + piece] = jnp.concatenate(
                        pair, axis=0
                    ).astype(BF16)
        for start in range(0, hid, tile):
            pre_act = jnp.dot(
                stacked_ref[...],
                in_ref[:, start : start + tile],
                preferred_element_type=jnp.float32,
            )
            hidden_grad = lax.dot_general(
                scaled_ref[...],
                out_ref[start : start + tile, :],
                (((1,), (1,)), ((), ())),
                preferred_element_type=jnp.float32,
            )
            sigmoid = jax.nn.sigmoid(pre_act)
            hidden_ref[:, start : start + tile] = (pre_act * sigmoid).astype(BF16)
            pre_grad_ref[:, start : start + tile] = (
                hidden_grad * sigmoid * (1.0 + pre_act * (1.0 - sigmoid))
            ).astype(BF16)
        for start in range(0, width, tile):
            returned = lax.dot_general(
                pre_grad_ref[...],
                in_ref[start : start + tile, :],
                (((1,), (1,)), ((), ())),
                preferred_element_type=jnp.float32,
            )
            for n in range(number):
                rows_back = returned[n * CAP : (n + 1) * CAP].astype(BF16)
                to = n // COLUMNS * width + start
                backs[n % COLUMNS][:, to : to + tile] = rows_back

    shapes = [(CAP, ring * width)] * COLUMNS
    shapes = shapes + [(rows, hid), (rows, width)]
    return pl.pallas_call(
        kernel,
        in_specs=[pl.BlockSpec(memory_space=pltpu.VMEM)] * (count + 2)
        + [pl.BlockSpec(memory_space=pltpu.SMEM)]
        + [pl.BlockSpec(memory_space=pl.ANY)] * len(after),
        out_specs=[pl.BlockSpec(memory_space=pltpu.VMEM)] * len(shapes),
        out_shape=[jax.ShapeDtypeStruct(shape, BF16) for shape in shapes],
        scratch_shapes=[pltpu.VMEM((rows, width), BF16), pltpu.VMEM((rows, hid), BF16)],
        cost_estimate=pl.CostEstimate(
            flops=6 * rows * width * hid,
            bytes_accessed=2 * (rows * width * 4 + 2 * width * hid),
            transcendentals=rows * hid,
        ),
        compiler_params=pltpu.CompilerParams(vmem_limit_bytes=40 * MIB),
    )(*arrays, weight_in, weight_out, me.reshape(1), *after)


def combine(placing, arrived, after=()):
    rows, tokens = placing.shape
    count = len(arrived)
    width = arrived[0].shape[1] // COLUMNS
    piece = 512

    def kernel(placing_ref, *refs):
        out_ref = refs[-1]
        for start in range(0, width, piece):
            stacked = jnp.concatenate(
                [
                    refs[d][:, c * width + start : c * width + start + piece].astype(jnp.float32)
                    for c in range(COLUMNS)
                    for d in range(count)
                ],
                axis=0,
            )
            out_ref[:, start : start + piece] = lax.dot_general(
                placing_ref[...],
                stacked.astype(BF16),
                (((0,), (0,)), ((), ())),
                preferred_element_type=jnp.float32,
            ).astype(BF16)

    return pl.pallas_call(
        kernel,
        in_specs=[pl.BlockSpec(memory_space=pltpu.VMEM)] * (count + 1)
        + [pl.BlockSpec(memory_space=pl.ANY)] * len(after),
        out_specs=pl.BlockSpec(memory_space=pltpu.VMEM),
        out_shape=jax.ShapeDtypeStruct((tokens, width), BF16),
        cost_estimate=pl.CostEstimate(
            flops=2 * rows * tokens * width,
            bytes_accessed=2 * (rows + tokens) * width,
            transcendentals=0,
        ),
        compiler_params=pltpu.CompilerParams(vmem_limit_bytes=24 * MIB),
    )(placing, *arrived, *after)


def weight_grad(hiddens, scaleds, after):
    rows, hid = hiddens[0].shape
    width = scaleds[0].shape[1]
    count = len(hiddens)
    tile = 512

    def kernel(*refs):
        out_ref = refs[-1]
        for start in range(0, hid, 256):
            total = None
            for hidden_ref, scaled_ref in zip(refs[:count], refs[count : 2 * count]):
                term = lax.dot_general(
                    hidden_ref[:, start : start + 256],
                    scaled_ref[...],
                    (((0,), (0,)), ((), ())),
                    preferred_element_type=jnp.float32,
                )
                total = term if total is None else total + term
            out_ref[start : start + 256, :] = total

    return pl.pallas_call(
        kernel,
        grid=(width // tile,),
        in_specs=[pl.BlockSpec((rows, hid), lambda i: (0, 0))] * count
        + [pl.BlockSpec((rows, tile), lambda i: (0, i))] * count
        + [pl.BlockSpec(memory_space=pl.ANY)] * len(after),
        out_specs=pl.BlockSpec((hid, tile), lambda i: (0, i)),
        out_shape=jax.ShapeDtypeStruct((hid, width), jnp.float32),
        cost_estimate=pl.CostEstimate(
            flops=2 * count * rows * hid * width,
            bytes_accessed=4 * hid * width + 2 * count * rows * (hid + width),
            transcendentals=0,
        ),
        compiler_params=pltpu.CompilerParams(vmem_limit_bytes=24 * MIB),
    )(*hiddens, *scaleds, *after)


def swap_groups(value):
    return lax.all_to_all(value, "expert", split_axis=0, concat_axis=0, tiled=True)


def shards(inputs, upstream, routes, gate_weights, proj_in, proj_out):
    groups = lax.axis_size("expert")
    ring = groups // COLUMNS
    local_count = EXPERTS // groups
    width = inputs.shape[3]
    weight_in = proj_in[0, 0]
    weight_out = proj_out[0, 0]
    me = lax.axis_index("expert")
    order = jnp.arange(groups, dtype=jnp.int32)
    place = (jnp.array(AWAY * COLUMNS, jnp.int32) + me) % ring
    near = (order // ring + me // ring) % COLUMNS * ring + place

    first = swap_groups(
        route_and_take(routes, gate_weights, inputs, upstream, 0, groups, local_count)
    )
    placing = build_slots(routes[0, 0], gate_weights[0, 0], near * local_count)[0]

    slots_1 = build_slots(routes[0, 1], gate_weights[0, 1], near * local_count)
    behind = from_behind(slots_1[0], "pipe", -1)
    own_rows, away_rows = slots_1[:, : ring * CAP], slots_1[:, ring * CAP :]

    def send_pack(start, stop):
        count = stop - start
        rows = slice(start * CAP, stop * CAP)
        away = swap_columns(take_rows(away_rows[:, rows], inputs, upstream, 1, True))
        own = take_rows(own_rows[:, rows], inputs, upstream, 1, True)
        moves = []
        for n in range(count):
            for c in range(COLUMNS):
                for part in range(2):
                    column = (part * count + n) * width
                    moves.append((c, column, n, (c * 2 + part) * width, width))
        return pack([own, away], moves, [4 * width] * count)

    blocks = send_pack(0, EARLY)
    second = {i: along_ring(blocks[i], AWAY[i]) for i in range(1, EARLY)}
    own_0, away_0, hidden_0, scaled_0 = expert_rows(first, me, weight_in, weight_out)
    held = (own_0, away_0, behind, placing, slots_1[0], send_pack(EARLY, ring))
    (own_0, away_0, behind, placing, _, late), second = together(held, second, range(1, EARLY))
    blocks += late
    second[0] = blocks[0]
    second.update({i: along_ring(blocks[i], AWAY[i]) for i in range(EARLY, ring)})
    back = pair_up(own_0, swap_columns(away_0), ring)
    rest = [i for i in range(1, ring) if i not in MEANWHILE]

    own_1, away_1, hidden_1, scaled_1 = expert_rows(
        [second[i] for i in range(ring)], me, weight_in, weight_out, back[:1]
    )
    back_0 = {i: along_ring(back[i], -AWAY[i]) for i in MEANWHILE}
    partial_value = weight_grad([hidden_0, hidden_1], [scaled_0, scaled_1], [])
    held = (own_1, away_1, [back[i] for i in rest])
    (own_1, away_1, held), back_0 = together(held, back_0, MEANWHILE)
    back_0.update({i: along_ring(held[n], -AWAY[i]) for n, i in enumerate(rest)})
    back_0[0] = back[0]
    held = (partial_value, swap_columns(away_1))
    (partial_value, away_1), back_0 = together(held, back_0, rest)
    back, partial_value = lax.optimization_barrier((pair_up(own_1, away_1, ring), partial_value))
    proj_grad = (partial_value + from_behind(partial_value, "dp", 1)).astype(BF16)
    back_1 = [along_ring_behind(back[i], -AWAY[i]) for i in LAST]
    back_1 = [back_1[LAST.index(i)] for i in range(ring)]

    grad_0 = from_behind(combine(placing, [back_0[i] for i in range(ring)]), "pipe", -1)
    grad_1 = combine(behind, back_1, [grad_0, proj_grad])
    return (jnp.stack([grad_0, grad_1])[None], proj_grad[None, None])


def solution(mesh):
    placed = (
        P("pipe", None, ("expert", "dp"), None),
        P("pipe", None, ("expert", "dp"), None),
        P("pipe", None, ("expert", "dp"), None),
        P("pipe", None, ("expert", "dp"), None),
        P("pipe", "expert", None, None),
        P("pipe", "expert", None, None),
    )
    return jax.shard_map(
        shards,
        mesh=mesh,
        in_specs=placed,
        out_specs=(P("pipe", None, ("expert", "dp"), None), P("pipe", "expert", None, None)),
        check_vma=False,
    )
```

```python
import functools

import jax
import jax.numpy as jnp
from jax import lax
from jax.experimental import pallas as pl
from jax.experimental.pallas import tpu as pltpu
from jax.sharding import PartitionSpec as P

EXPERTS = 128
CAP = 24
COLUMNS = 2
AWAY = (0, 4, 1, 7, 2, 6, 3, 5)
EARLY = 4
MEANWHILE = (2, 3, 4, 5)
BEFORE = (4, 5, 6, 7)
BF16 = jnp.bfloat16
MIB = 1024 * 1024


def from_behind(value, axis, steps):
    count = lax.axis_size(axis)
    pairs = [(source, (source + steps) % count) for source in range(count)]
    return lax.ppermute(value, axis, pairs)


def swap_columns(value):
    return from_behind(value, "expert", lax.axis_size("expert") // COLUMNS)


def swap_columns_behind(value):
    sections, groups = lax.axis_size("pipe"), lax.axis_size("expert")
    pairs = [
        (s * groups + e, (s - 1) % sections * groups + (e + groups // COLUMNS) % groups)
        for s in range(sections)
        for e in range(groups)
    ]
    return lax.ppermute(value, ("pipe", "expert"), pairs)


def along_ring(value, steps):
    groups = lax.axis_size("expert")
    ring = groups // COLUMNS
    pairs = [(e, e // ring * ring + (e + steps) % ring) for e in range(groups)]
    return lax.ppermute(value, "expert", pairs)


def together(held, blocks, positions):
    held, arrived = lax.optimization_barrier((held, [blocks[i] for i in positions]))
    return held, {**blocks, **dict(zip(positions, arrived))}


def build_slots(route_ids, gate_rows, experts):
    matches = route_ids[:, :, None] == experts
    routed = jnp.any(matches, axis=1)
    weight = jnp.sum(jnp.where(matches, gate_rows.astype(jnp.float32)[:, :, None], 0.0), axis=1)
    slot_rank = jnp.cumsum(routed.astype(jnp.int32), axis=0) - 1
    slot_ids = jnp.arange(CAP, dtype=jnp.int32)
    chosen = routed.T[:, None, :] & (slot_rank.T[:, None, :] == slot_ids[None, :, None])
    placing = chosen.astype(BF16)
    gated = jnp.where(chosen, weight.T[:, None, :], 0.0).astype(BF16)
    return jnp.stack([placing, gated]).reshape(2, experts.shape[0] * CAP, -1)


def take_rows(slots, inputs, upstream, micro, side_by_side):
    _, rows, tokens = slots.shape
    width = inputs.shape[3]
    blocks = rows // CAP
    piece = 512
    tile = width if side_by_side else width // 2
    tiles = width // tile

    def kernel(slots_ref, inputs_ref, upstream_ref, out_ref):
        def take(rows_ref):
            for start in range(0, tile, piece):
                taken = jnp.dot(
                    slots_ref[0],
                    rows_ref[0, 0, :, start : start + piece],
                    preferred_element_type=jnp.float32,
                )
                for n in range(blocks):
                    block = taken[n * CAP : (n + 1) * CAP].astype(BF16)
                    if side_by_side:
                        out_ref[:, n * width + start : n * width + start + piece] = block
                    else:
                        out_ref[n, :, start : start + piece] = block

        @pl.when(pl.program_id(0) < tiles)
        def _():
            take(inputs_ref)

        @pl.when(pl.program_id(0) >= tiles)
        def _():
            take(upstream_ref)

    if side_by_side:
        out_spec = pl.BlockSpec((CAP, blocks * width), lambda i: (0, i))
        out_shape = (CAP, 2 * blocks * width)
    else:
        out_spec = pl.BlockSpec((blocks, CAP, tile), lambda i: (0, 0, i))
        out_shape = (blocks, CAP, 2 * width)
    return pl.pallas_call(
        kernel,
        grid=(2 * tiles,),
        in_specs=[
            pl.BlockSpec((1, rows, tokens), lambda i: (i // tiles, 0, 0)),
            pl.BlockSpec((1, 1, tokens, tile), lambda i: (0, micro, 0, jnp.minimum(i, tiles - 1))),
            pl.BlockSpec((1, 1, tokens, tile), lambda i: (0, micro, 0, jnp.maximum(i - tiles, 0))),
        ],
        out_specs=out_spec,
        out_shape=pltpu.HBM(out_shape, BF16),
        cost_estimate=pl.CostEstimate(
            flops=4 * rows * tokens * width,
            bytes_accessed=4 * width * (rows + tokens),
            transcendentals=0,
        ),
        compiler_params=pltpu.CompilerParams(vmem_limit_bytes=24 * MIB),
    )(slots, inputs, upstream)


def route_and_take(routes, gate_weights, inputs, upstream, micro, groups, local_count):
    tokens, width = inputs.shape[2:]
    top = routes.shape[3]
    rows = groups * CAP
    piece = 512
    tile = width // 2
    tiles = width // tile

    def kernel(routes_ref, gate_ref, inputs_ref, upstream_ref, out_ref, slots_ref):
        @pl.when(pl.program_id(0) == 0)
        def _():
            experts = routes_ref[0, 0].astype(jnp.float32)
            gates = gate_ref[0, 0].astype(jnp.float32)
            targets = lax.broadcasted_iota(jnp.int32, (groups, tokens), 0) * local_count
            targets = targets.astype(jnp.float32)
            routed = jnp.zeros((groups, tokens), jnp.float32)
            weight = jnp.zeros((groups, tokens), jnp.float32)
            for k in range(top):
                match = experts[k : k + 1] == targets
                routed = jnp.where(match, 1.0, routed)
                weight = weight + jnp.where(match, gates[k : k + 1], 0.0)
            upto = jnp.where(
                lax.broadcasted_iota(jnp.int32, (tokens, tokens), 0)
                <= lax.broadcasted_iota(jnp.int32, (tokens, tokens), 1),
                1.0,
                0.0,
            ).astype(BF16)
            rank = jnp.dot(routed.astype(BF16), upto, preferred_element_type=jnp.float32)
            slot = jnp.where(routed > 0.5, rank, 0.0)
            ids = lax.broadcasted_iota(jnp.int32, (CAP, tokens), 0).astype(jnp.float32) + 1.0
            for n in range(0, groups, 2):
                chosen = [slot[n + k : n + k + 1] == ids for k in range(2)]
                ones = [jnp.where(pick, 1.0, 0.0) for pick in chosen]
                gated = [
                    jnp.where(pick, weight[n + k : n + k + 1], 0.0) for k, pick in enumerate(chosen)
                ]
                at = slice(n * CAP, (n + 2) * CAP)
                slots_ref[0, at, :] = jnp.concatenate(ones, axis=0).astype(BF16)
                slots_ref[1, at, :] = jnp.concatenate(gated, axis=0).astype(BF16)

        def take(which, rows_ref):
            for start in range(0, tile, piece):
                taken = jnp.dot(
                    slots_ref[which],
                    rows_ref[0, 0, :, start : start + piece],
                    preferred_element_type=jnp.float32,
                )
                for n in range(groups):
                    block = taken[n * CAP : (n + 1) * CAP].astype(BF16)
                    out_ref[n, :, start : start + piece] = block

        @pl.when(pl.program_id(0) < tiles)
        def _():
            take(0, inputs_ref)

        @pl.when(pl.program_id(0) >= tiles)
        def _():
            take(1, upstream_ref)

    return pl.pallas_call(
        kernel,
        grid=(2 * tiles,),
        in_specs=[
            pl.BlockSpec((1, 1, top, tokens), lambda i: (0, micro, 0, 0)),
            pl.BlockSpec((1, 1, top, tokens), lambda i: (0, micro, 0, 0)),
            pl.BlockSpec((1, 1, tokens, tile), lambda i: (0, micro, 0, jnp.minimum(i, tiles - 1))),
            pl.BlockSpec((1, 1, tokens, tile), lambda i: (0, micro, 0, jnp.maximum(i - tiles, 0))),
        ],
        out_specs=pl.BlockSpec((groups, CAP, tile), lambda i: (0, 0, i)),
        out_shape=pltpu.HBM((groups, CAP, 2 * width), BF16),
        scratch_shapes=[pltpu.VMEM((2, rows, tokens), BF16)],
        cost_estimate=pl.CostEstimate(
            flops=4 * rows * tokens * width,
            bytes_accessed=4 * width * (rows + tokens),
            transcendentals=0,
        ),
        compiler_params=pltpu.CompilerParams(vmem_limit_bytes=24 * MIB),
    )(
        jnp.swapaxes(routes, 2, 3),
        jnp.swapaxes(gate_weights, 2, 3),
        pltpu.with_memory_space_constraint(inputs, pltpu.HBM),
        pltpu.with_memory_space_constraint(upstream, pltpu.HBM),
    )


def pack(arrays, moves, out_widths, after=()):
    count, outs = len(arrays) + len(after), len(out_widths)

    def kernel(*refs):
        sources, targets = refs[:count], refs[count : count + outs]
        buffers, in_sems, out_sems = refs[count + outs : -2], refs[-2], refs[-1]
        reads = [
            pltpu.make_async_copy(
                sources[a].at[:, pl.ds(start, size)],
                buffers[o].at[:, pl.ds(to, size)],
                in_sems.at[n],
            )
            for n, (a, start, o, to, size) in enumerate(moves)
        ]
        writes = [
            pltpu.make_async_copy(buffers[o], targets[o], out_sems.at[o]) for o in range(outs)
        ]
        for read in reads:
            read.start()
        for o in range(outs):
            for read, move in zip(reads, moves):
                if move[2] == o:
                    read.wait()
            writes[o].start()
        for write in writes:
            write.wait()

    total = sum(out_widths) * CAP * 2
    shapes = [(CAP, size) for size in out_widths]
    return pl.pallas_call(
        kernel,
        in_specs=[pl.BlockSpec(memory_space=pl.ANY)] * count,
        out_specs=[pl.BlockSpec(memory_space=pl.ANY)] * outs,
        out_shape=[jax.ShapeDtypeStruct(shape, BF16) for shape in shapes],
        scratch_shapes=[pltpu.VMEM(shape, BF16) for shape in shapes]
        + [pltpu.SemaphoreType.DMA((len(moves),)), pltpu.SemaphoreType.DMA((outs,))],
        cost_estimate=pl.CostEstimate(flops=0, bytes_accessed=2 * total, transcendentals=0),
        compiler_params=pltpu.CompilerParams(vmem_limit_bytes=16 * MIB),
    )(*arrays, *after)


def pair_up(arrays, ring):
    size = arrays[0].shape[1] // ring
    moves = [
        (n, d * size, d, n * size, size) for d in range(ring) for n in range(len(arrays))
    ]
    return pack(arrays, moves, [len(arrays) * size] * ring)


def expert_rows(blocks, me, weight_in, weight_out, cuts, after=()):
    width, hid = weight_in.shape
    one = not isinstance(blocks, list)
    arrays = [blocks] if one else blocks
    count = len(arrays)
    number = blocks.shape[0] if one else COLUMNS * count
    rows = number * CAP
    tile = 256
    piece = 512
    ring = number // COLUMNS
    share = width // cuts

    def kernel(*refs):
        in_ref, out_ref, me_ref = refs[count : count + 3]
        backs = refs[count + 3 + len(after) :][: COLUMNS * cuts]
        mine, place = me_ref[0] // ring, me_ref[0] % ring
        hidden_ref, scaled_ref, stacked_ref, pre_grad_ref = refs[-4:]

        def block(n, column):
            columns = slice(column, column + piece)
            if one:
                source = (mine + n) % COLUMNS * ring + (place + ring - AWAY[n // COLUMNS]) % ring
                return refs[0][source, :, columns]
            shift = n % COLUMNS * 2 * width
            return refs[n // COLUMNS][:, column + shift : column + shift + piece]

        for n in range(0, number, 2):
            for target_ref, first in ((stacked_ref, 0), (scaled_ref, width)):
                for start in range(0, width, piece):
                    pair = [block(n + k, first + start).astype(jnp.float32) for k in range(2)]
                    target_ref[n * CAP : (n + 2) * CAP, start : start + piece] = jnp.concatenate(
                        pair, axis=0
                    ).astype(BF16)
        for start in range(0, hid, tile):
            pre_act = jnp.dot(
                stacked_ref[...],
                in_ref[:, start : start + tile],
                preferred_element_type=jnp.float32,
            )
            hidden_grad = lax.dot_general(
                scaled_ref[...],
                out_ref[start : start + tile, :],
                (((1,), (1,)), ((), ())),
                preferred_element_type=jnp.float32,
            )
            sigmoid = jax.nn.sigmoid(pre_act)
            hidden_ref[:, start : start + tile] = (pre_act * sigmoid).astype(BF16)
            pre_grad_ref[:, start : start + tile] = (
                hidden_grad * sigmoid * (1.0 + pre_act * (1.0 - sigmoid))
            ).astype(BF16)
        for start in range(0, width, tile):
            returned = lax.dot_general(
                pre_grad_ref[...],
                in_ref[start : start + tile, :],
                (((1,), (1,)), ((), ())),
                preferred_element_type=jnp.float32,
            )
            for n in range(number):
                rows_back = returned[n * CAP : (n + 1) * CAP].astype(BF16)
                to = n // COLUMNS * share + start % share
                backs[start // share * COLUMNS + n % COLUMNS][:, to : to + tile] = rows_back

    shapes = [(CAP, ring * share)] * (COLUMNS * cuts)
    shapes = shapes + [(rows, hid), (rows, width)]
    return pl.pallas_call(
        kernel,
        in_specs=[pl.BlockSpec(memory_space=pltpu.VMEM)] * (count + 2)
        + [pl.BlockSpec(memory_space=pltpu.SMEM)]
        + [pl.BlockSpec(memory_space=pl.ANY)] * len(after),
        out_specs=[pl.BlockSpec(memory_space=pltpu.VMEM)] * len(shapes),
        out_shape=[jax.ShapeDtypeStruct(shape, BF16) for shape in shapes],
        scratch_shapes=[pltpu.VMEM((rows, width), BF16), pltpu.VMEM((rows, hid), BF16)],
        cost_estimate=pl.CostEstimate(
            flops=6 * rows * width * hid,
            bytes_accessed=2 * (rows * width * 4 + 2 * width * hid),
            transcendentals=rows * hid,
        ),
        compiler_params=pltpu.CompilerParams(vmem_limit_bytes=40 * MIB),
    )(*arrays, weight_in, weight_out, me.reshape(1), *after)


def combine(placing, arrived, first, width, after=()):
    rows, tokens = placing.shape
    count = len(arrived)
    piece = 512

    def kernel(placing_ref, *refs):
        out_ref = refs[-1]
        for start in range(0, width, piece):
            stacked = jnp.concatenate(
                [
                    refs[d][:, column : column + piece].astype(jnp.float32)
                    for column in (first + start, first + width + start)
                    for d in range(count)
                ],
                axis=0,
            )
            out_ref[:, start : start + piece] = lax.dot_general(
                placing_ref[...],
                stacked.astype(BF16),
                (((0,), (0,)), ((), ())),
                preferred_element_type=jnp.float32,
            ).astype(BF16)

    return pl.pallas_call(
        kernel,
        in_specs=[pl.BlockSpec(memory_space=pltpu.VMEM)] * (count + 1)
        + [pl.BlockSpec(memory_space=pl.ANY)] * len(after),
        out_specs=pl.BlockSpec(memory_space=pltpu.VMEM),
        out_shape=jax.ShapeDtypeStruct((tokens, width), BF16),
        cost_estimate=pl.CostEstimate(
            flops=2 * rows * tokens * width,
            bytes_accessed=2 * (rows + tokens) * width,
            transcendentals=0,
        ),
        compiler_params=pltpu.CompilerParams(vmem_limit_bytes=24 * MIB),
    )(placing, *arrived, *after)


def weight_grad(hiddens, scaleds, after):
    rows, hid = hiddens[0].shape
    width = scaleds[0].shape[1]
    count = len(hiddens)
    tile = 512

    def kernel(*refs):
        out_ref = refs[-1]
        for start in range(0, hid, 256):
            total = None
            for hidden_ref, scaled_ref in zip(refs[:count], refs[count : 2 * count]):
                term = lax.dot_general(
                    hidden_ref[:, start : start + 256],
                    scaled_ref[...],
                    (((0,), (0,)), ((), ())),
                    preferred_element_type=jnp.float32,
                )
                total = term if total is None else total + term
            out_ref[start : start + 256, :] = total

    return pl.pallas_call(
        kernel,
        grid=(width // tile,),
        in_specs=[pl.BlockSpec((rows, hid), lambda i: (0, 0))] * count
        + [pl.BlockSpec((rows, tile), lambda i: (0, i))] * count
        + [pl.BlockSpec(memory_space=pl.ANY)] * len(after),
        out_specs=pl.BlockSpec((hid, tile), lambda i: (0, i)),
        out_shape=jax.ShapeDtypeStruct((hid, width), jnp.float32),
        cost_estimate=pl.CostEstimate(
            flops=2 * count * rows * hid * width,
            bytes_accessed=4 * hid * width + 2 * count * rows * (hid + width),
            transcendentals=0,
        ),
        compiler_params=pltpu.CompilerParams(vmem_limit_bytes=24 * MIB),
    )(*hiddens, *scaleds, *after)


def swap_groups(value):
    return lax.all_to_all(value, "expert", split_axis=0, concat_axis=0, tiled=True)


def shards(inputs, upstream, routes, gate_weights, proj_in, proj_out):
    groups = lax.axis_size("expert")
    ring = groups // COLUMNS
    local_count = EXPERTS // groups
    width = inputs.shape[3]
    weight_in = proj_in[0, 0]
    weight_out = proj_out[0, 0]
    me = lax.axis_index("expert")
    order = jnp.arange(groups, dtype=jnp.int32)
    place = (jnp.array(AWAY * COLUMNS, jnp.int32) + me) % ring
    near = (order // ring + me // ring) % COLUMNS * ring + place

    first = swap_groups(
        route_and_take(routes, gate_weights, inputs, upstream, 0, groups, local_count)
    )
    placing = build_slots(routes[0, 0], gate_weights[0, 0], near * local_count)[0]

    slots_1 = build_slots(routes[0, 1], gate_weights[0, 1], near * local_count)
    behind = from_behind(slots_1[0], "pipe", -1)
    own_rows, away_rows = slots_1[:, : ring * CAP], slots_1[:, ring * CAP :]

    def send_pack(start, stop):
        count = stop - start
        rows = slice(start * CAP, stop * CAP)
        away = swap_columns(take_rows(away_rows[:, rows], inputs, upstream, 1, True))
        own = take_rows(own_rows[:, rows], inputs, upstream, 1, True)
        moves = []
        for n in range(count):
            for c in range(COLUMNS):
                for part in range(2):
                    column = (part * count + n) * width
                    moves.append((c, column, n, (c * 2 + part) * width, width))
        return pack([own, away], moves, [4 * width] * count)

    blocks = send_pack(0, EARLY)
    second = {i: along_ring(blocks[i], AWAY[i]) for i in range(1, EARLY)}
    own_0, away_0, hidden_0, scaled_0 = expert_rows(first, me, weight_in, weight_out, 1)
    held = (own_0, away_0, behind, placing, slots_1[0], send_pack(EARLY, ring))
    (own_0, away_0, behind, placing, placing_1, late), second = together(held, second, range(1, EARLY))
    blocks += late
    second[0] = blocks[0]
    second.update({i: along_ring(blocks[i], AWAY[i]) for i in range(EARLY, ring)})
    back = pair_up([own_0, swap_columns(away_0)], ring)
    rest = [i for i in range(1, ring) if i not in MEANWHILE]

    *cut_1, hidden_1, scaled_1 = expert_rows(
        [second[i] for i in range(ring)], me, weight_in, weight_out, 2, back[:1]
    )
    back_0 = {i: along_ring(back[i], -AWAY[i]) for i in MEANWHILE}
    held = (cut_1, [back[i] for i in rest])
    (cut_1, held), back_0 = together(held, back_0, MEANWHILE)
    back_0.update({i: along_ring(held[n], -AWAY[i]) for n, i in enumerate(rest)})
    back_0[0] = back[0]
    partial_value = weight_grad([hidden_0, hidden_1], [scaled_0, scaled_1], [])
    own_left, away_left, own_right, away_right = cut_1
    moved = [
        own_left,
        swap_columns(away_left),
        from_behind(own_right, "pipe", -1),
        swap_columns_behind(away_right),
    ]
    (partial_value, moved), back_0 = together((partial_value, moved), back_0, rest)
    back = pair_up(moved, ring)
    back_1 = {i: along_ring(back[i], -AWAY[i]) for i in range(1, ring)}
    back_1[0] = back[0]

    grad_0 = combine(placing, [back_0[i] for i in range(ring)], 0, width)
    (grad_0, partial_value), back_1 = together((grad_0, partial_value), back_1, BEFORE)
    back_1 = [back_1[i] for i in range(ring)]
    grad_0 = from_behind(grad_0, "pipe", -1)
    proj_grad = (partial_value + from_behind(partial_value, "dp", 1)).astype(BF16)
    left = combine(placing_1, back_1, 0, width // 2, [grad_0, proj_grad])
    right = combine(behind, back_1, width, width // 2, [left])
    left = from_behind(left, "pipe", -1)
    grad_1 = jnp.concatenate([left, right], axis=1)
    return (jnp.stack([grad_0, grad_1])[None], proj_grad[None, None])


def solution(mesh):
    placed = (
        P("pipe", None, ("expert", "dp"), None),
        P("pipe", None, ("expert", "dp"), None),
        P("pipe", None, ("expert", "dp"), None),
        P("pipe", None, ("expert", "dp"), None),
        P("pipe", "expert", None, None),
        P("pipe", "expert", None, None),
    )
    return jax.shard_map(
        shards,
        mesh=mesh,
        in_specs=placed,
        out_specs=(P("pipe", None, ("expert", "dp"), None), P("pipe", "expert", None, None)),
        check_vma=False,
    )
```
